32 devices in a mesh: section: 2 (over core), dp: 16 (over z, y, x).
Axes of the slice: x: 2, y: 2, z: 4, core: 2. Of those that a mesh axis runs over, the one named last changes fastest.
Arguments:
- patches: bfloat16 [32, 24, 24, 1024], P('dp'), may hold values from -6 to 6
- grid_counts: int32 [16], P('dp'), may hold values from 1 to 2, as said below
- reduce_w: bfloat16 [2, 1024, 1024], P('section'), may hold values from -0.1875 to 0.1875
- conv_w: bfloat16 [2, 9, 1024, 1024], P('section'), may hold values from -0.0625 to 0.0625
- expand_w: bfloat16 [2, 1024, 1024], P('section'), may hold values from -0.1875 to 0.1875
- norm_gain: float32 [2, 3072], P('section'), may hold values from 0.25 to 1.75
- norm_bias: float32 [2, 3072], P('section'), may hold values from -1.8 to 1.8
- readout_w: bfloat16 [1024, 4096], replicated, may hold values from -0.1875 to 0.1875
- readout_b: float32 [4096], replicated, may hold values from -1.8 to 1.8
- out_grad: bfloat16 [32, 12, 12, 4096], P('dp'), may hold values from -6 to 6
Outputs:
- mixed: bfloat16 [32, 12, 12, 4096], P('dp', None, None, 'section')
- patch_grad: bfloat16 [32, 24, 24, 1024], P('dp', None, None, 'section')
- grad_reduce: float32 [2, 1024, 1024], P('section', 'dp')
- grad_conv: float32 [2, 9216, 1024], P('section', None, 'dp')
- grad_expand: float32 [2, 1024, 1024], P('section', None, 'dp')
- grad_norm: float32 [2, 6144], P('section', 'dp')
- grad_readout: float32 [1024, 4096], P(None, ('section', 'dp'))
- grad_readout_bias: float32 [4096], P(('section', 'dp'))
The draws below stay inside these ranges and needn't reach their ends.
Inputs may be any that keep to these rules, and one draw needn't show every extreme that they name: `grid_counts`: the 1 images of one dp device have at most 2 grids together; in every draw some device has exactly 2.
All inputs are finite; a program needn't handle non-finite values.
Results may differ from the reference program's by a relative error of at most 0.018.
Values may be sent and summed in bfloat16 or wider, within the bound.
A program may use at most 576 MiB of HBM per device.

```python
import jax
import jax.numpy as jnp
from jax import lax

D = 1024
MID = 1024
R = 4096
SIDE = 24
POOLED = 12
IMG_DEV = 1
CAP = 2
GRIDS = 32
IMAGES = 16
N_DP = 16


def draw_grid_counts(key, part):
    key = jax.random.fold_in(key, 7)
    key_first, key_device = jax.random.split(key, 2)
    devices = IMAGES // IMG_DEV
    counts = jax.random.randint(key_first, (devices,), 1, CAP + 1)
    chosen = jax.random.randint(key_device, (), 0, devices)
    picked = jnp.arange(devices) == chosen
    counts = jnp.where(picked, CAP, counts)
    return counts.reshape(-1).astype(jnp.int32)


def with_spikes(array, stream_key, source, target, shards_of, factor):
    owner, partner = [(jnp.arange(array.shape[axis_at]) // (array.shape[axis_at] // shards_of)).reshape([-1 if axis == axis_at else 1 for axis in range(array.ndim)]) for axis_at in (source, target)]
    chosen = jax.random.permutation(stream_key, shards_of)[partner]
    strong = (owner == chosen) | (owner == (partner + shards_of // 2) % shards_of)
    return jnp.where(strong, factor * array, array)


def block_levels(stream_key, extent, shards, smallest, top_value):
    level, own = 1.0, jax.random.fold_in(stream_key, 6)
    for axis_at, blocks in shards:
        steps = jnp.exp(jax.random.uniform(jax.random.fold_in(own, axis_at), (blocks,), jnp.float32, smallest / len(shards), top_value / len(shards)))
        level = level * jnp.repeat(steps, extent[axis_at] // blocks).reshape([-1 if axis == axis_at else 1 for axis in range(len(extent))])
    return level


def gaussian(own_key, dims, scale, reach, pieces=(), dtype=jnp.bfloat16):
    loudness = block_levels(own_key, dims, pieces, -0.22, 0.18) if pieces else 1.0
    array = jax.random.normal(own_key, dims, jnp.float32) * scale * loudness
    return jnp.minimum(jnp.maximum(array, -reach), reach).astype(dtype)


def noise_with(own_key, shape, scale, bound, cuts, heavy, held_as=jnp.bfloat16):
    entries = scale * jax.random.normal(own_key, shape, jnp.float32)
    if cuts:
        entries = entries * block_levels(own_key, shape, cuts, -0.22, 0.18)
    return jnp.clip(with_spikes(entries, jax.random.fold_in(own_key, 3), *heavy), -bound, bound).astype(held_as)


def setup_inputs(seed: int = 0) -> dict:
    streams_of = jax.random.split(jax.random.key(seed), 11)
    patches = noise_with(streams_of[0], (GRIDS, SIDE, SIDE, D), 1.0, 6.0, ((0, 16),), (0, 3, 16, 2.0))
    grid_counts = draw_grid_counts(jax.random.fold_in(streams_of[10], 71), 0)
    reduce_w = gaussian(streams_of[2], (2, D, MID), D ** -0.5, 0.1875, ((0, 2),))
    conv_w = gaussian(streams_of[3], (2, 9, MID, MID), (9 * MID) ** -0.5, 0.0625, ((0, 2),))
    expand_w = gaussian(streams_of[4], (2, MID, D), MID ** -0.5, 0.1875, ((0, 2),))
    norm_gain = jnp.clip(1.0 + 0.15 * jax.random.normal(streams_of[5], (2, 2 * MID + D), jnp.float32), 0.25, 1.75)
    norm_bias = gaussian(streams_of[6], (2, 2 * MID + D), 0.3, 1.8, ((0, 2),), jnp.float32)
    readout_w = gaussian(streams_of[7], (D, R), D ** -0.5, 0.1875)
    readout_b = gaussian(streams_of[8], (R,), 0.3, 1.8, (), jnp.float32)
    out_grad = noise_with(streams_of[9], (GRIDS, POOLED, POOLED, R), 1.0, 6.0, ((0, 16),), (0, 3, 16, 2.0))
    return {"patches": patches, "grid_counts": grid_counts, "reduce_w": reduce_w, "conv_w": conv_w, "expand_w": expand_w, "norm_gain": norm_gain, "norm_bias": norm_bias, "readout_w": readout_w, "readout_b": readout_b, "out_grad": out_grad}


@jax.custom_vjp
def low(v):
    return lax.optimization_barrier(v.astype(jnp.bfloat16)).astype(jnp.float32)

@jax.custom_vjp
def low_back(v):
    return v

def low_keep(v):
    return (low(v), None)

def low_pass(kept, grad):
    return (grad,)

def back_keep(v):
    return (v, None)

def back_low(kept, grad):
    return (low(grad),)
low.defvjp(low_keep, low_pass)
low_back.defvjp(back_keep, back_low)
norm_epsilon = 1e-05
highest = lax.Precision.HIGHEST

def norm_silu(values, scale_vec, shift_vec):
    average = lax.optimization_barrier(jnp.mean(values, axis=-1, keepdims=True))
    centered = values - average
    variance = lax.optimization_barrier(jnp.mean(centered * centered, axis=-1, keepdims=True))
    return jax.nn.silu(centered * lax.rsqrt(variance + norm_epsilon) * scale_vec + shift_vec)

def conv_cells(activity, conv_weights):
    grid_side = activity.shape[1]
    padded = jnp.pad(activity, ((0, 0), (1, 1), (1, 1), (0, 0)))
    summed = None
    for tap_index in range(9):
        vertical = tap_index // 3
        lateral = tap_index % 3
        window = padded[:, vertical:vertical + grid_side, lateral:lateral + grid_side, :]
        partial_sum = jnp.einsum('gijc,cd->gijd', window, conv_weights[tap_index], precision=highest)
        summed = partial_sum if summed is None else summed + partial_sum
    return summed

def block(inputs, reduce_weights, conv_weights, expand_weights, gains, biases):
    middle = reduce_weights.shape[1]
    first_pre = low_back(jnp.einsum('gijc,cd->gijd', inputs, reduce_weights, precision=highest))
    first_act = low(norm_silu(first_pre, gains[:middle], biases[:middle]))
    conv_pre = low_back(conv_cells(first_act, conv_weights))
    conv_act = low(norm_silu(conv_pre, gains[middle:2 * middle], biases[middle:2 * middle]))
    expand_pre = low_back(jnp.einsum('gijc,cd->gijd', conv_act, expand_weights, precision=highest))
    return inputs + norm_silu(expand_pre, gains[2 * middle:], biases[2 * middle:])

def pool_cells(values):
    grids, grid_side, _, channels = values.shape
    half_side = grid_side // 2
    return values.reshape(grids, half_side, 2, half_side, 2, channels).mean(axis=(2, 4))

def forward(params, grids, slot_mask):
    reduce_all, conv_all, expand_all, gain_all, bias_all, readout_weights, readout_bias = params
    first_out = block(grids, reduce_all[0], conv_all[0], expand_all[0], gain_all[0], bias_all[0])
    pooled = low_back(low(pool_cells(first_out)))
    second_out = block(pooled, reduce_all[1], conv_all[1], expand_all[1], gain_all[1], bias_all[1])
    readout_pre = low_back(jnp.einsum('gijd,dr->gijr', low(second_out), readout_weights, precision=highest) + readout_bias)
    return jax.nn.gelu(readout_pre, approximate=False) * slot_mask[:, None, None, None]

def reference(patches, grid_counts, reduce_w, conv_w, expand_w, norm_gain, norm_bias, readout_w, readout_b, out_grad):
    params = (reduce_w.astype(jnp.float32), conv_w.astype(jnp.float32), expand_w.astype(jnp.float32), norm_gain.astype(jnp.float32), norm_bias.astype(jnp.float32), readout_w.astype(jnp.float32), readout_b.astype(jnp.float32))
    images = patches.astype(jnp.float32).reshape(N_DP, CAP, SIDE, SIDE, D)
    cotangents = out_grad.astype(jnp.float32).reshape(N_DP, CAP, POOLED, POOLED, R)
    live_grids = lax.optimization_barrier(jnp.sum(grid_counts.reshape(N_DP, IMG_DEV), axis=1))
    masks = (jnp.arange(CAP)[None, :] < live_grids[:, None]).astype(jnp.float32)

    def one_device(running, inputs):
        grids, cotangent, slot_mask = inputs
        produced, pullback = jax.vjp(lambda values, cells: forward(values, cells, slot_mask), params, grids)
        param_grads, grid_grads = pullback(cotangent)
        running = jax.tree.map(jnp.add, running, param_grads)
        return (running, (produced.astype(jnp.bfloat16), grid_grads.astype(jnp.bfloat16)))
    totals, (mixed, patch_grads) = lax.scan(one_device, jax.tree.map(jnp.zeros_like, params), (images, cotangents, masks))
    grad_scale = 1.0 / N_DP
    grad_norm = jnp.concatenate([totals[3], totals[4]], axis=1) * grad_scale
    return (mixed.reshape(GRIDS, POOLED, POOLED, R), patch_grads.reshape(GRIDS, SIDE, SIDE, D), totals[0] * grad_scale, totals[1].reshape(2, 9 * MID, MID) * grad_scale, totals[2] * grad_scale, grad_norm, totals[5] * grad_scale, totals[6] * grad_scale)
```

```python
import functools

import jax
import jax.numpy as jnp
from jax import lax
from jax.experimental import pallas as pl
from jax.experimental.pallas import tpu as pltpu
from jax.sharding import PartitionSpec as P

BF = jnp.bfloat16
F32 = jnp.float32
EPSILON = 1e-05
VMEM_BYTES = 60 * 2**20
READOUT_TILE = 512


def dot_nn(a, b):
    return lax.dot_general(a, b, (((1,), (0,)), ((), ())), preferred_element_type=F32)


def dot_nt(a, b):
    return lax.dot_general(a, b, (((1,), (1,)), ((), ())), preferred_element_type=F32)


def norm_stats(h):
    mean = jnp.mean(h, axis=-1, keepdims=True)
    centered = h - mean
    var = jnp.mean(centered * centered, axis=-1, keepdims=True)
    inv = lax.rsqrt(var + EPSILON)
    return centered * inv, inv


def norm_act(h, gain, bias):
    n, _ = norm_stats(h)
    o = n * gain + bias
    return 0.5 * o * (1.0 + jnp.tanh(0.5 * o))


def norm_pull(dy, h, gain, bias):
    n, inv = norm_stats(h)
    o = n * gain + bias
    s = 0.5 + 0.5 * jnp.tanh(0.5 * o)
    t = dy * (s * (1.0 + o * (1.0 - s)))
    tg = t * gain
    mean_tg = jnp.mean(tg, axis=-1, keepdims=True)
    mean_tgn = jnp.mean(tg * n, axis=-1, keepdims=True)
    return (tg - mean_tg - n * mean_tgn) * inv, t, t * n


def row_loop(rows, body, step=16, unroll=12):
    count = rows // step
    while count % unroll:
        unroll -= 1

    def run(i, carry):
        body(pl.multiple_of(i * step, step))
        return carry

    lax.fori_loop(0, count, run, 0, unroll=unroll)


def fold8(v):
    return jnp.sum(v.reshape(v.shape[0] // 8, 8, v.shape[1]), axis=0)


class Geometry:
    def __init__(self, grids, side, extra=0):
        self.grids = grids
        self.side = side
        self.stride = grids * side
        self.rows = self.stride * side
        self.split = self.stride % 16 != 0
        self.copies = 2 if self.split else 1
        self.extra = extra
        self.padded = self.rows + 2 * self.stride + extra

    def tap_shape(self, channels):
        return (3 * self.copies, self.padded, channels)

    def tap(self, taps, u, v, rows=None):
        rows = self.rows if rows is None else rows
        if not self.split:
            return taps[v, pl.ds(pl.multiple_of(u * self.stride, 16), rows), :]
        middle = (u == 1).astype(jnp.int32)
        start = pl.multiple_of((1 - middle) * u * self.stride, 16)
        return taps[middle * 3 + v, pl.ds(start, rows), :]

    def fill(self, flat, taps):
        channels = taps.shape[-1]
        width = 256
        chunk = 48
        for copy in range(self.copies):
            first = copy * self.stride
            count = (self.padded - 2 * first) // chunk

            def run(k, carry):
                row = pl.multiple_of(k * chunk, chunk)
                for column in range(0, channels, width):
                    c = pl.ds(column, width)
                    a = flat[pl.ds(pl.multiple_of(first + row, 8), chunk), c]
                    j = lax.broadcasted_iota(jnp.int32, a.shape, 0) % self.side
                    r = pl.ds(row, chunk)
                    taps[3 * copy, r, c] = jnp.where(j == 0, 0.0, pltpu.roll(a, 1, 0)).astype(BF)
                    taps[3 * copy + 1, r, c] = a.astype(BF)
                    taps[3 * copy + 2, r, c] = jnp.where(
                        j == self.side - 1, 0.0, pltpu.roll(a, chunk - 1, 0)
                    ).astype(BF)
                return carry

            lax.fori_loop(0, count, run, 0, unroll=1)

    def clear(self, flat):
        flat[pl.ds(0, self.stride), :] = jnp.zeros((self.stride, flat.shape[-1]), flat.dtype)
        tail = self.stride + self.extra
        flat[pl.ds(self.stride + self.rows, tail), :] = jnp.zeros((tail, flat.shape[-1]), flat.dtype)


def constant(shape):
    return pl.BlockSpec(shape, lambda t: (0,) * len(shape), pipeline_mode=pl.Buffered(1))


ANY = pl.BlockSpec(memory_space=pl.ANY)


def copies_out(pairs, sems):
    return [pltpu.make_async_copy(src, dst, sems.at[i]) for i, (src, dst) in enumerate(pairs)]


def first_forward_kernel(
    geo, x_ref, wr_ref, wc_ref, we_ref, gain_ref, bias_ref,
    a1_out, a2_out, h1_out, h2_out, h3_out, z_ref,
    taps, flat, h1, h2, h3, a2, zf, sems,
):
    t = pl.program_id(0)
    on = lax.axis_index("section") == 0
    rows, stride, side = geo.rows, geo.stride, geo.side
    gain = [gain_ref[k : k + 1, :] for k in range(3)]
    bias = [bias_ref[k : k + 1, :] for k in range(3)]
    out = copies_out(
        [(a2, a2_out), (h1, h1_out), (h2, h2_out), (h3, h3_out), (taps.at[1, pl.ds(stride, rows)], a1_out)], sems
    )

    @pl.when(on & (t == 0))
    def _():
        h1[...] = dot_nn(x_ref[...], wr_ref[...])
        out[1].start()
        geo.clear(flat)

        def body(r):
            flat[pl.ds(stride + r, 16), :] = norm_act(h1[pl.ds(r, 16), :], gain[0], bias[0])

        row_loop(rows, body)
        geo.fill(flat, taps)
        out[4].start()
        h2[...] = jnp.zeros_like(h2)

    @pl.when(on & (t >= 1) & (t <= 9))
    def _():
        tap = t - 1
        h2[...] += dot_nn(geo.tap(taps, tap // 3, tap % 3), wc_ref[0])

    @pl.when(on & (t == 10))
    def _():
        out[2].start()

        def body(r):
            a2[pl.ds(r, 16), :] = norm_act(h2[pl.ds(r, 16), :], gain[1], bias[1]).astype(BF)

        row_loop(rows, body)
        out[0].start()
        h3[...] = dot_nn(a2[...], we_ref[...])
        out[3].start()

        def pool(i, carry):
            total = None
            for k in range(2):
                r = pl.ds(pl.multiple_of((2 * i + k) * stride, stride), stride)
                y = x_ref[r, :].astype(F32) + norm_act(h3[r, :], gain[2], bias[2])
                total = y if total is None else total + y
            total = total + pltpu.roll(total, stride - 1, 0)
            pairs = total.reshape(stride // 2, 2, total.shape[1])[:, 0, :]
            zf[pl.ds(pl.multiple_of(i * side, 8), side), :] = pairs * 0.25
            return carry

        lax.fori_loop(0, side // 2, pool, 0, unroll=2)
        z_ref[...] = zf[...].astype(BF)
        for c in out:
            c.wait()


def first_forward(geo, x, wr, wc, we, gain, bias):
    rows, channels = x.shape
    middle = wr.shape[1]
    small = rows // 4
    return pl.pallas_call(
        functools.partial(first_forward_kernel, geo),
        grid=(11,),
        in_specs=[
            constant((rows, channels)), constant((channels, middle)),
            pl.BlockSpec((1, middle, middle), lambda t: (jnp.clip(t - 1, 0, 8), 0, 0)),
            constant((middle, channels)), constant(gain.shape), constant(bias.shape),
        ],
        out_specs=[ANY] * 5 + [constant((small, channels))],
        out_shape=[
            jax.ShapeDtypeStruct((rows, middle), BF), jax.ShapeDtypeStruct((rows, middle), BF),
            jax.ShapeDtypeStruct((rows, middle), F32), jax.ShapeDtypeStruct((rows, middle), F32),
            jax.ShapeDtypeStruct((rows, channels), F32), jax.ShapeDtypeStruct((small, channels), BF),
        ],
        scratch_shapes=[
            pltpu.VMEM(geo.tap_shape(middle), BF), pltpu.VMEM((geo.padded, middle), F32),
            pltpu.VMEM((rows, middle), F32), pltpu.VMEM((rows, middle), F32), pltpu.VMEM((rows, channels), F32),
            pltpu.VMEM((rows, middle), BF), pltpu.VMEM((small, channels), F32), pltpu.SemaphoreType.DMA((5,)),
        ],
        compiler_params=pltpu.CompilerParams(vmem_limit_bytes=VMEM_BYTES),
        cost_estimate=pl.CostEstimate(flops=22 * rows * channels * middle, bytes_accessed=40 * 2**20, transcendentals=0),
        name="first_forward",
    )(x, wr, wc, we, gain, bias)


def second_forward_kernel(
    geo, tiles, live_ref, z_ref, wr_ref, wc_ref, we_ref, gain_ref, bias_ref, wro_ref, rb_ref, og_ref,
    a1_ref, a2_ref, h1, h2, h3, y_ref, dy_ref, mixed_ref, dpre_ref, gb_ref,
    taps, flat,
):
    t = pl.program_id(0)
    on = lax.axis_index("section") == 1
    rows, stride = geo.rows, geo.stride
    gain = [gain_ref[k : k + 1, :] for k in range(3)]
    bias = [bias_ref[k : k + 1, :] for k in range(3)]

    @pl.when(on & (t == 0))
    def _():
        h1[...] = dot_nn(z_ref[...], wr_ref[...])
        geo.clear(flat)

        def body(r):
            a = norm_act(h1[pl.ds(r, 16), :], gain[0], bias[0])
            flat[pl.ds(stride + r, 16), :] = a
            a1_ref[pl.ds(r, 16), :] = a.astype(BF)

        row_loop(rows, body)
        geo.fill(flat, taps)
        h2[...] = jnp.zeros_like(h2)

    @pl.when(on & (t >= 1) & (t <= 9))
    def _():
        tap = t - 1
        h2[...] += dot_nn(geo.tap(taps, tap // 3, tap % 3), wc_ref[0])

    @pl.when(on & (t == 10))
    def _():
        def body(r):
            a2_ref[pl.ds(r, 16), :] = norm_act(h2[pl.ds(r, 16), :], gain[1], bias[1]).astype(BF)

        row_loop(rows, body)
        h3[...] = dot_nn(a2_ref[...], we_ref[...])

        def last(r):
            y = z_ref[pl.ds(r, 16), :].astype(F32) + norm_act(h3[pl.ds(r, 16), :], gain[2], bias[2])
            y_ref[pl.ds(r, 16), :] = y.astype(BF)

        row_loop(rows, last)
        dy_ref[...] = jnp.zeros_like(dy_ref)

    @pl.when(on & (t >= 11))
    def _():
        pre = dot_nn(y_ref[...], wro_ref[...]) + rb_ref[...]
        slot = lax.broadcasted_iota(jnp.int32, (rows, 1), 0) % stride // geo.side
        mask = jnp.where(slot < live_ref[0], 1.0, 0.0)
        phi = 0.5 + 0.5 * lax.erf(pre * 0.7071067811865476)
        mixed_ref[...] = (pre * phi * mask).astype(BF)
        density = jnp.exp(-0.5 * pre * pre) * 0.3989422804014327
        low = (og_ref[...].astype(F32) * mask * (phi + pre * density)).astype(BF)
        dpre_ref[...] = low
        gb_ref[...] = jnp.sum(low.astype(F32), axis=0, keepdims=True)
        dy_ref[...] += dot_nt(low, wro_ref[...])


def second_forward(geo, live, z, wr, wc, we, gain, bias, wro, rb, og):
    rows, channels = z.shape
    middle = wr.shape[1]
    units = wro.shape[1]
    tile = READOUT_TILE
    tiles = units // tile

    def at(t):
        return jnp.clip(t - 11, 0, tiles - 1)

    def rowsof(dtype, width=middle):
        return jax.ShapeDtypeStruct((rows, width), dtype)

    return pl.pallas_call(
        functools.partial(second_forward_kernel, geo, tiles),
        grid=(11 + tiles,),
        in_specs=[
            pl.BlockSpec(memory_space=pltpu.SMEM),
            constant((rows, channels)), constant((channels, middle)),
            pl.BlockSpec((1, middle, middle), lambda t: (jnp.clip(t - 1, 0, 8), 0, 0)),
            constant((middle, channels)), constant(gain.shape), constant(bias.shape),
            pl.BlockSpec((channels, tile), lambda t: (0, at(t))),
            pl.BlockSpec((1, tile), lambda t: (0, at(t))),
            pl.BlockSpec((rows, tile), lambda t: (0, at(t))),
        ],
        out_specs=[constant((rows, middle))] * 7
        + [pl.BlockSpec((rows, tile), lambda t: (0, at(t)))] * 2 + [pl.BlockSpec((1, tile), lambda t: (0, at(t)))],
        out_shape=[
            rowsof(BF), rowsof(BF), rowsof(F32), rowsof(F32), rowsof(F32), rowsof(BF), rowsof(F32),
            rowsof(BF, units), rowsof(BF, units), jax.ShapeDtypeStruct((1, units), F32),
        ],
        scratch_shapes=[pltpu.VMEM(geo.tap_shape(middle), BF), pltpu.VMEM((geo.padded, middle), F32)],
        compiler_params=pltpu.CompilerParams(vmem_limit_bytes=VMEM_BYTES),
        cost_estimate=pl.CostEstimate(flops=40 * rows * channels * middle, bytes_accessed=40 * 2**20, transcendentals=0),
        name="second_forward",
    )(live, z, wr, wc, we, gain, bias, wro, rb, og)


def backward_kernel(
    geo, section, pooled, d_ref, h1_in, h2_in, h3_in, wr_ref, wc_ref, we_ref, gain_ref, bias_ref,
    dh3_out, dh2_out, dh1_out, dx_ref, norm_ref,
    taps, flat, h1, h2, h3, low, dy, sems, sems_out,
):
    t = pl.program_id(0)
    on = lax.axis_index("section") == section
    rows, stride, side = geo.rows, geo.stride, geo.side
    gain = [gain_ref[k : k + 1, :] for k in range(3)]
    bias = [bias_ref[k : k + 1, :] for k in range(3)]
    loads = [pltpu.make_async_copy(s, d, sems.at[i]) for i, (s, d) in enumerate([(h3_in, h3), (h2_in, h2), (h1_in, h1)])]
    out3, out2, out1 = copies_out([(low.at[0], dh3_out), (low.at[1], dh2_out), (low.at[2], dh1_out)], sems_out)

    def pull(k, source, h, store):
        norm_ref[k] = jnp.zeros_like(norm_ref[k])
        norm_ref[3 + k] = jnp.zeros_like(norm_ref[k])

        def body(r):
            dh, tt, tn = norm_pull(source[pl.ds(r, 16), :], h[pl.ds(r, 16), :], gain[k], bias[k])
            store(r, dh)
            norm_ref[k] += fold8(tn)
            norm_ref[3 + k] += fold8(tt)

        row_loop(rows, body, unroll=9)

    @pl.when(on & (t == 0))
    def _():
        for c in loads:
            c.start()
        if pooled:
            half = side // 2
            grids = stride // side
            narrow = grids * half
            flat[pl.ds(0, half * narrow), :] = d_ref[...].astype(F32)
            a = lax.broadcasted_iota(jnp.int32, (stride, narrow), 0) // 2
            b = lax.broadcasted_iota(jnp.int32, (stride, narrow), 1)
            quarter = jnp.where(a == b, 0.25, 0.0).astype(BF)

            def widen(i, carry):
                part = flat[pl.ds(pl.multiple_of(i * narrow, 8), narrow), :].astype(BF)
                wide = dot_nn(quarter, part)
                for k in range(2):
                    dy[pl.ds(pl.multiple_of((2 * i + k) * stride, stride), stride), :] = wide
                return carry

            lax.fori_loop(0, half, widen, 0, unroll=2)
        else:
            dy[...] = d_ref[...]
        loads[0].wait()

        def store3(r, v):
            low[0, pl.ds(r, 16), :] = v.astype(BF)

        pull(2, dy, h3, store3)
        out3.start()
        h3[...] = dot_nt(low[0], we_ref[...])
        loads[1].wait()
        geo.clear(flat)

        def store2(r, v):
            low[1, pl.ds(r, 16), :] = v.astype(BF)
            flat[pl.ds(stride + r, 16), :] = v

        pull(1, h3, h2, store2)
        out2.start()
        geo.fill(flat, taps)
        h2[...] = jnp.zeros_like(h2)

    @pl.when(on & (t >= 1) & (t <= 9))
    def _():
        tap = t - 1
        h2[...] += dot_nt(geo.tap(taps, tap // 3, tap % 3), wc_ref[0])

    @pl.when(on & (t == 10))
    def _():
        loads[2].wait()

        def store1(r, v):
            low[2, pl.ds(r, 16), :] = v.astype(BF)

        pull(0, h2, h1, store1)
        out1.start()
        dx_ref[...] = (dy[...] + dot_nt(low[2], wr_ref[...])).astype(BF)
        for c in (out3, out2, out1):
            c.wait()


def backward(geo, section, pooled, d, h1, h2, h3, wr, wc, we, gain, bias):
    rows = geo.rows
    channels, middle = wr.shape
    low = jax.ShapeDtypeStruct((rows, middle), BF)
    return pl.pallas_call(
        functools.partial(backward_kernel, geo, section, pooled),
        grid=(11,),
        in_specs=[
            constant(d.shape), ANY, ANY, ANY, constant((channels, middle)),
            pl.BlockSpec((1, middle, middle), lambda t: (8 - jnp.clip(t - 1, 0, 8), 0, 0)),
            constant((middle, channels)), constant(gain.shape), constant(bias.shape),
        ],
        out_specs=[ANY] * 3 + [constant((rows, channels)), constant((6, 8, channels))],
        out_shape=[low, low, low, jax.ShapeDtypeStruct((rows, channels), BF), jax.ShapeDtypeStruct((6, 8, channels), F32)],
        scratch_shapes=[
            pltpu.VMEM(geo.tap_shape(middle), BF), pltpu.VMEM((geo.padded, middle), F32),
            pltpu.VMEM((rows, middle), F32), pltpu.VMEM((rows, middle), F32), pltpu.VMEM((rows, channels), F32),
            pltpu.VMEM((3, rows, middle), BF), pltpu.VMEM((rows, channels), F32),
            pltpu.SemaphoreType.DMA((3,)), pltpu.SemaphoreType.DMA((3,)),
        ],
        compiler_params=pltpu.CompilerParams(vmem_limit_bytes=VMEM_BYTES),
        cost_estimate=pl.CostEstimate(flops=22 * rows * channels * middle, bytes_accessed=40 * 2**20, transcendentals=0),
        name="backward",
    )(d, h1, h2, h3, wr, wc, we, gain, bias)


class Scatter:
    def __init__(self, size, rows):
        self.size = size
        self.bits = size.bit_length() - 1
        self.block = max(rows // size, 16)
        self.low = (self.block * size // rows).bit_length() - 1
        self.high = self.bits - self.low

    def exchange(self, x, bit):
        return lax.ppermute(x, "dp", [(i, i ^ (1 << bit)) for i in range(self.size)])

    def run(self, send, keep, order):
        units, _, columns = send.shape
        left = [b for b in reversed(range(self.high)) if b != order[0]]
        shape = (units,) + (2,) * len(left) + (self.block, columns)
        send, keep = send.reshape(shape), keep.reshape(shape)
        for step, bit in enumerate(order):
            got = self.exchange(send, bit + self.low)
            if step + 1 == len(order):
                total = got.astype(F32) + keep.astype(F32)
                break
            axis = 1 + left.index(order[step + 1])
            left.remove(order[step + 1])

            def half(v, k):
                return lax.index_in_dim(v, k, axis, keepdims=False).astype(F32)

            send = (half(got, 1) + half(keep, 1)).astype(BF)
            keep = half(got, 0) + half(keep, 0)
        total = total.reshape(units, self.block, columns)
        for bit in reversed(range(self.low)):
            pair = total.reshape(units, 2, total.shape[1] // 2, columns)
            mine = (lax.axis_index("dp") >> bit) & 1
            send = jnp.where(mine == 0, pair[:, 1], pair[:, 0])
            total = jnp.where(mine == 0, pair[:, 0], pair[:, 1])
            total = total + self.exchange(send.astype(BF), bit).astype(F32)
        return total


def turn(lhs, turned, block, flip):
    def run(q, carry):
        part = jnp.transpose(lhs[:, pl.ds(pl.multiple_of(q * 128, 128), 128)])
        step = min(block, 128)
        for s in range(128 // step):
            row = q * 128 + s * step
            target = ((row // block) ^ flip) * block + row % block
            turned[pl.ds(pl.multiple_of(target, 16), step), :] = part[s * step : (s + 1) * step]
        return carry

    lax.fori_loop(0, lhs.shape[1] // 128, run, 0, unroll=1)


def store_halves(value, send, keep, block, bit):
    run = block << bit
    for i in range(value.shape[0] // run):
        target = keep if i % 2 == 0 else send
        target[0, pl.ds(i // 2 * run, run), :] = value[i * run : (i + 1) * run].astype(BF)


def fetch(own, pairs, sems):
    @pl.when(own)
    def _():
        cs = [pltpu.make_async_copy(a, t, sems.at[i]) for i, (a, b, t) in enumerate(pairs)]
        for c in cs:
            c.start()
        for c in cs:
            c.wait()

    @pl.when(jnp.logical_not(own))
    def _():
        cs = [pltpu.make_async_copy(b, t, sems.at[i]) for i, (a, b, t) in enumerate(pairs)]
        for c in cs:
            c.start()
        for c in cs:
            c.wait()


GROUPS = ((0, 4, 0), (4, 4, 1), (8, 3, 2))


def block_grads_kernel(
    geo, section, scatter, *refs
):
    names = ("a1", "a2", "dh3", "dh2", "dh1")
    own_refs, got_refs = refs[0:5], refs[5:10]
    x_ref = refs[10]
    outs = refs[11:17]
    right, wide, flat, taps, turned, sems = refs[17:]
    own = lax.axis_index("section") == section
    mine = lax.axis_index("section")
    flip = lax.axis_index("dp") // (1 << scatter.low)
    t = pl.program_id(0)
    rows, stride = geo.rows, geo.stride
    depth = wide.shape[0]
    width = right.shape[1]
    columns = pl.ds(pl.multiple_of(mine * width, width), width)

    def load(right_name, wide_name):
        k = names.index(right_name)
        pairs = [(own_refs[k].at[:, columns], got_refs[k].at[:, columns], right.at[pl.ds(0, rows)])]
        if wide_name is not None:
            j = names.index(wide_name)
            pairs.append((own_refs[j], got_refs[j], wide.at[pl.ds(0, rows)]))
        else:
            pairs.append((x_ref, x_ref, wide.at[pl.ds(0, rows)]))
        fetch(own, pairs, sems)

    def emit(value, group):
        store_halves(value, outs[2 * group], outs[2 * group + 1], scatter.block, GROUPS[group][2])

    @pl.when(t == 0)
    def _():
        if depth > rows:
            wide[pl.ds(rows, depth - rows), :] = jnp.zeros((depth - rows, wide.shape[1]), BF)
            right[pl.ds(rows, depth - rows), :] = jnp.zeros((depth - rows, width), BF)
        load("a1", "dh2")
        geo.clear(flat)

        def body(r):
            flat[pl.ds(stride + r, 16), :] = right[pl.ds(r, 16), :].astype(F32)

        row_loop(rows, body)
        geo.fill(flat, taps)
        turn(wide, turned, scatter.block, flip)

    for group, (first, count, _) in enumerate(GROUPS):
        @pl.when((t >= first) & (t < min(first + count, 9)))
        def _():
            value = dot_nn(turned[...], geo.tap(taps, t // 3, t % 3, depth))
            emit(value, group)

    for step, names_used in ((9, ("a2", "dh3")), (10, ("dh1", None))):
        @pl.when(t == step)
        def _():
            load(*names_used)
            turn(wide, turned, scatter.block, flip)
            emit(dot_nn(turned[...], right[...]), 2)


def block_grads(geo, section, size, own, got, x):
    rows, channels = x.shape
    scatter = Scatter(size, channels)
    width = channels // 2
    depth = -(-rows // 128) * 128
    geo = Geometry(geo.grids, geo.side, depth - rows)
    half = channels // 2

    def group_spec(first, count):
        return pl.BlockSpec((1, half, width), lambda t: (jnp.clip(t - first, 0, count - 1), 0, 0))

    specs, shapes = [], []
    for first, count, _ in GROUPS:
        specs += [group_spec(first, count)] * 2
        shapes += [jax.ShapeDtypeStruct((count, half, width), BF)] * 2
    outs = pl.pallas_call(
        functools.partial(block_grads_kernel, geo, section, scatter),
        grid=(11,),
        in_specs=[ANY] * 11,
        out_specs=specs,
        out_shape=shapes,
        scratch_shapes=[
            pltpu.VMEM((depth, width), BF), pltpu.VMEM((depth, channels), BF), pltpu.VMEM((geo.padded, width), F32),
            pltpu.VMEM(geo.tap_shape(width), BF), pltpu.VMEM((channels, depth), BF), pltpu.SemaphoreType.DMA((2,)),
        ],
        compiler_params=pltpu.CompilerParams(vmem_limit_bytes=VMEM_BYTES),
        cost_estimate=pl.CostEstimate(flops=11 * rows * channels * channels, bytes_accessed=20 * 2**20, transcendentals=0),
        name="block_grads",
    )(*own, *got, x)
    orders = {0: [0, 1], 1: [1, 0], 2: [2, 3]}
    results = []
    for g, (_, _, bit) in enumerate(GROUPS):
        head = orders[bit]
        order = head + [b for b in range(scatter.high) if b not in head]
        if bit == 2:
            order = [b for b in range(2, scatter.high)] + [0, 1]
        results.append(scatter.run(outs[2 * g], outs[2 * g + 1], order))
    return jnp.concatenate(results, axis=0)


def readout_grads_kernel(
    rows, scatter, y_own, y_got, d_own, d_got, send0, keep0, send1, keep1, right, wide, turned, sems
):
    own = lax.axis_index("section") == 1
    mine = lax.axis_index("section")
    t = pl.program_id(0)
    depth, width = right.shape
    columns = pl.ds(pl.multiple_of(mine * width, width), width)

    @pl.when(t == 0)
    def _():
        if depth > rows:
            wide[pl.ds(rows, depth - rows), :] = jnp.zeros((depth - rows, wide.shape[1]), BF)
            right[pl.ds(rows, depth - rows), :] = jnp.zeros((depth - rows, width), BF)
        fetch(own, [(y_own.at[:, columns], y_got.at[:, columns], right.at[pl.ds(0, rows)]),
                    (d_own, d_got, wide.at[pl.ds(0, rows)])], sems)
        turn(wide, turned, scatter.block, lax.axis_index("dp"))

    part = turned.shape[0] // 4
    for s, (send, keep) in enumerate(((send0, keep0), (send1, keep1))):
        @pl.when(t // 2 == s)
        def _():
            value = dot_nn(turned[pl.ds(pl.multiple_of(t * part, part), part), :], right[...])
            store_halves(value, send, keep, scatter.block, s)


def readout_grads(size, y_own, y_got, d_own, d_got):
    rows, channels = y_own.shape
    units = d_own.shape[1]
    scatter = Scatter(size, units // 2)
    width = channels // 2
    depth = -(-rows // 128) * 128
    half = units // 8
    out = jax.ShapeDtypeStruct((2, half, width), BF)
    specs = [pl.BlockSpec((1, half, width), lambda t: (jnp.clip(t, 0, 1), 0, 0))] * 2
    specs += [pl.BlockSpec((1, half, width), lambda t: (jnp.clip(t - 2, 0, 1), 0, 0))] * 2
    outs = pl.pallas_call(
        functools.partial(readout_grads_kernel, rows, scatter),
        grid=(4,),
        in_specs=[ANY] * 4,
        out_specs=specs,
        out_shape=[out] * 4,
        scratch_shapes=[
            pltpu.VMEM((depth, width), BF), pltpu.VMEM((depth, units), BF), pltpu.VMEM((units, depth), BF),
            pltpu.SemaphoreType.DMA((2,)),
        ],
        compiler_params=pltpu.CompilerParams(vmem_limit_bytes=VMEM_BYTES),
        cost_estimate=pl.CostEstimate(flops=rows * channels * units, bytes_accessed=12 * 2**20, transcendentals=0),
        name="readout_grads",
    )(y_own, y_got, d_own, d_got)
    rest = list(range(2, scatter.high))
    results = []
    for s, head in enumerate(([0, 1], [1, 0])):
        send, keep = (v.reshape(1, 2 * half, width) for v in outs[2 * s : 2 * s + 2])
        results.append(scatter.run(send, keep, head + rest))
    return jnp.concatenate(results, axis=0)


def to_section(x, target):
    return lax.ppermute(x, "section", [(1 - target, target)])


def swap_sections(x):
    return lax.ppermute(x, "section", [(0, 1), (1, 0)])


def side_by_side(v):
    grids, side, _, channels = v.shape
    return v.transpose(1, 0, 2, 3).reshape(grids * side * side, channels)


def by_grid(v, grids, side):
    return v.reshape(side, grids, side, v.shape[-1]).transpose(1, 0, 2, 3)


def on_device(
    size, patches, grid_counts, reduce_w, conv_w, expand_w, norm_gain, norm_bias, readout_w, readout_b, out_grad
):
    section = lax.axis_index("section")
    is_first = section == 0
    grids, side, _, channels = patches.shape
    middle = reduce_w.shape[2]
    units = readout_w.shape[1]
    wide, small = Geometry(grids, side), Geometry(grids, side // 2)
    weights = (reduce_w[0], conv_w[0], expand_w[0], norm_gain.reshape(3, channels), norm_bias.reshape(3, channels))
    live = jnp.sum(grid_counts, dtype=jnp.int32).reshape(1)
    x = side_by_side(patches)
    cotangent = side_by_side(out_grad)

    a1, a2, h1, h2, h3, z = first_forward(wide, x, *weights)
    z_got = to_section(z, 1)
    z_all = jnp.where(is_first, z, z_got)
    first_got = [to_section(v, 1) for v in (a1, a2)]
    b1, b2, k1, k2, k3, y, dy, mixed_full, dpre, bias_sum = second_forward(
        small, live, z_got, *weights, readout_w, readout_b.reshape(1, units), cotangent
    )
    y_got, dpre_got = to_section(y, 0), to_section(dpre, 0)
    second_got = [to_section(v, 0) for v in (b1, b2)]
    e3, e2, e1, dz, norm_second = backward(small, 1, False, dy, k1, k2, k3, *weights)
    dz_got = to_section(dz, 0)
    second_got += [to_section(v, 0) for v in (e3, e2, e1)]
    readout_part = readout_grads(size, y, y_got, dpre, dpre_got)
    second_part = block_grads(small, 1, size, (b1, b2, e3, e2, e1), second_got, z_all)
    d3, d2, d1, dx, norm_first = backward(wide, 0, True, dz_got, h1, h2, h3, *weights)
    first_got += [to_section(v, 1) for v in (d3, d2, d1)]
    first_part = block_grads(wide, 0, size, (a1, a2, d3, d2, d1), first_got, x)

    scale = 1.0 / size
    block_part = jnp.where(is_first, first_part, second_part)
    other = swap_sections(jnp.where(is_first, second_part, first_part))
    block_total = jnp.where(
        is_first, jnp.concatenate([block_part, other], axis=2), jnp.concatenate([other, block_part], axis=2)
    ) * scale
    rows = block_total.shape[1]
    conv_total = block_total[:9].transpose(0, 2, 1).reshape(1, 9 * middle, rows)
    expand_total = block_total[9].T[None]
    reduce_total = block_total[10][None]
    mine = jnp.where(is_first, readout_part[0], readout_part[1])
    other = swap_sections(jnp.where(is_first, readout_part[1], readout_part[0]))
    readout_total = jnp.where(
        is_first, jnp.concatenate([mine, other], axis=1), jnp.concatenate([other, mine], axis=1)
    ).T * scale

    norms = jnp.where(is_first, norm_first, norm_second).sum(axis=1).reshape(size, -1)
    share = norms.shape[1]
    biases = bias_sum.reshape(2, size, -1)
    vectors = jnp.concatenate([norms, biases[0], biases[1]], axis=1)
    vectors = lax.psum_scatter(vectors, "dp", scatter_dimension=0, tiled=True)[0] * scale
    count = biases.shape[2]
    low = to_section(vectors[share : share + count], 0)
    bias_total = jnp.where(is_first, low, vectors[share + count :])

    low = to_section(mixed_full[:, : units // 2], 0)
    mixed = by_grid(jnp.where(is_first, low, mixed_full[:, units // 2 :]), grids, side // 2)
    high = to_section(dx[:, channels // 2 :], 1)
    patch_grad = by_grid(jnp.where(is_first, dx[:, : channels // 2], high), grids, side)
    return (
        mixed, patch_grad, reduce_total, conv_total, expand_total, vectors[None, :share], readout_total, bias_total,
    )


def solution(mesh):
    size = mesh.shape["dp"]
    placed = (
        P("dp", None, None, None), P("dp"), P("section", None, None), P("section", None, None, None),
        P("section", None, None), P("section", None), P("section", None), P(), P(), P("dp", None, None, None),
    )
    return jax.shard_map(
        functools.partial(on_device, size),
        mesh=mesh,
        in_specs=placed,
        out_specs=(
            P("dp", None, None, "section"), P("dp", None, None, "section"), P("section", "dp", None),
            P("section", None, "dp"), P("section", None, "dp"), P("section", "dp"), P(None, ("section", "dp")),
            P(("section", "dp")),
        ),
        check_vma=False,
    )
```
